32 devices in a mesh: groups: 2 (over x), dp: 16 (over z, y, core).
Axes of the slice: x: 2, y: 2, z: 4, core: 2. Of those that a mesh axis runs over, the one named last changes fastest.
Arguments:
- hidden: bfloat16 [128, 96, 5120], P(('groups', 'dp')), parts along dimension 0
- exit_gain: float32 [5120], replicated, may hold values from 0.5 to 1.5
- exit_weight: bfloat16 [5120, 10240], P(None, 'dp')
- labels: int32 [128], P('groups'), parts along dimension 0, may hold values from 0 to 10239
- exit_ids: int32 [64], P('groups'), parts along dimension 0, may hold values from 0 to 63, as said below
- destination: int32 [128], P('groups'), parts along dimension 0, may hold values from 0 to 15, as said below
Outputs:
- exit_nll: float32 [128], P(('groups', 'dp')), parts along dimension 0
- exit_bins: float32 [128, 15], P(('groups', 'dp')), parts along dimension 0
- moved_rows: bfloat16 [64, 96, 5120], P(('groups', 'dp')), parts along dimension 0
The draws below stay inside these ranges and needn't reach their ends.
There are 2 independent parts, one for each index of `groups`. The reference program is written for one: setup_inputs(seed, part) draws one part's arguments, and reference() takes and returns one part's arrays. A program takes and returns all parts, laid end to end along the dimension named above; an argument that names none is the same for every part. Nothing has to cross between parts.
Inputs may be any that keep to these rules, and one draw needn't show every extreme that they name: `exit_ids`: 32 distinct prompt ids in no particular order. A prompt's destination is its own shard (prompts p with p // 4 as shard) or a shard next to it; a prompt in exit_ids has its own shard; from one shard at most one surviving prompt goes to each neighbour, and every shard receives exactly 2 surviving prompts.
All inputs are finite; a program needn't handle non-finite values.
Results may differ from the reference program's by a relative error of at most 0.0019.
The reference program's roundings to bfloat16 on the way (of `normed`) count: a program that leaves them out, or rounds other values in their place, can miss the bound.
Values may be sent and summed in bfloat16 or wider, within the bound.
A program may use at most 128 MiB of HBM per device.

```python
import math
import jax
import jax.numpy as jnp
from jax import lax

D = 5120
PROMPT_DEV = 4
LEN = 96
BINS = 15
SURV_DEV = 2
PROMPTS = 64
SURVIVING_COUNT = 32
EXITS = 32
VOCAB = 10240
N_DP = 16


def route_plan(key):
    right_neighbour_key, key_left, key_rank = jax.random.split(key, 3)
    shard_ids = jnp.arange(N_DP, dtype=jnp.int32)
    to_right = (jax.random.randint(right_neighbour_key, (N_DP,), 0, 4) < 3).astype(jnp.int32)
    to_left = (jax.random.randint(key_left, (N_DP,), 0, 4) < 3).astype(jnp.int32)
    to_right = jnp.where(shard_ids == 0, 1, jnp.where(shard_ids == N_DP - 1, 0, to_right))
    to_left = jnp.where(shard_ids == 0, 0, jnp.where(shard_ids == N_DP - 1, 1, to_left))
    from_left = jnp.concatenate([jnp.zeros((1,), jnp.int32), to_right[:-1]])
    from_right = jnp.concatenate([to_left[1:], jnp.zeros((1,), jnp.int32)])
    staying = SURV_DEV - from_left - from_right
    subkeys = jax.random.split(key_rank, N_DP)
    rank_table = jax.vmap(lambda subkey: jax.random.permutation(subkey, PROMPT_DEV))(subkeys).astype(jnp.int32)
    column = shard_ids[:, None]
    goal_shard = jnp.where(rank_table < to_left[:, None], column - 1, jnp.where(rank_table < (to_left + to_right)[:, None], column + 1, jnp.where(rank_table < (to_left + to_right + staying)[:, None], column, -1)))
    return goal_shard.reshape(PROMPTS).astype(jnp.int32)


def draw_destination(key, part):
    goal_shard = route_plan(key)
    home_shard = jnp.arange(PROMPTS, dtype=jnp.int32) // PROMPT_DEV
    return jnp.where(goal_shard < 0, home_shard, goal_shard).astype(jnp.int32)


def draw_exit_ids(key, part):
    goal_shard = route_plan(key)
    key = jax.random.fold_in(key, 41)
    prompt_ids = jnp.arange(PROMPTS, dtype=jnp.int32)
    sorting_key = jnp.where(goal_shard < 0, prompt_ids, PROMPTS + prompt_ids)
    chosen = jnp.argsort(sorting_key)[:EXITS].astype(jnp.int32)
    return jax.random.permutation(key, chosen).astype(jnp.int32)


def draw_hidden(key, part):
    key = jax.random.fold_in(key, 11)
    base_draw = jax.random.normal(key, (PROMPTS, LEN, D), jnp.float32)
    return base_draw.astype(jnp.bfloat16)


def draw_exit_weight(key, part):
    key = jax.random.fold_in(key, 23)
    weight_scale = 3.0 / D ** 0.5
    base_draw = jax.random.normal(key, (D, VOCAB), jnp.float32) * weight_scale
    return base_draw.astype(jnp.bfloat16)


def with_ends(entries, rng, smallest, largest):
    extent = entries.shape
    index_at = [jax.random.randint(jax.random.fold_in(rng, axis), (), 0, extent[axis]) for axis in range(len(extent))]
    entries = entries.at[tuple(index_at)].set(smallest)
    longest = extent.index(max(extent))
    index_at[longest] = (index_at[longest] + 1) % extent[longest]
    return entries.at[tuple(index_at)].set(largest)


def setup_inputs(seed: int = 0, part: int = 0) -> dict:
    splits = jax.random.split(jax.random.key(seed), 7)
    own_keys = jax.random.split(jax.random.fold_in(splits[6], part), 7)
    hidden = draw_hidden(jax.random.fold_in(jax.random.fold_in(splits[6], part), 71), part)
    exit_gain = jnp.clip(1.0 + 0.1 * jax.random.normal(splits[1], (D,), jnp.float32), 0.5, 1.5)
    exit_weight = draw_exit_weight(jax.random.fold_in(splits[6], 71), part)
    labels = with_ends(jax.random.randint(own_keys[3], (PROMPTS,), 0, VOCAB), jax.random.fold_in(own_keys[3], 1), 0, VOCAB - 1).astype(jnp.int32)
    exit_ids = draw_exit_ids(jax.random.fold_in(jax.random.fold_in(splits[6], part), 71), part)
    destination = draw_destination(jax.random.fold_in(jax.random.fold_in(splits[6], part), 71), part)
    return {"hidden": hidden, "exit_gain": exit_gain, "exit_weight": exit_weight, "labels": labels, "exit_ids": exit_ids, "destination": destination}


epsilon = 1e-06

def reference(hidden, exit_gain, exit_weight, labels, exit_ids, destination):
    final_rows = hidden[:, -1, :].astype(jnp.float32)
    mean_square = lax.optimization_barrier(jnp.mean(final_rows * final_rows, axis=1, keepdims=True))
    normed = (final_rows * lax.rsqrt(mean_square + epsilon) * exit_gain.astype(jnp.float32)).astype(jnp.bfloat16)
    logits = jnp.dot(normed, exit_weight, preferred_element_type=jnp.float32)
    peak_value = lax.optimization_barrier(jnp.max(logits, axis=1))
    exponent_sum = lax.optimization_barrier(jnp.sum(jnp.exp(logits - peak_value[:, None]), axis=1))
    log_total = peak_value + jnp.log(exponent_sum)
    label_logit = jnp.take_along_axis(logits, labels[:, None].astype(jnp.int32), axis=1)[:, 0]
    exit_nll = log_total - label_logit
    bin_place = BINS * (1.0 + (peak_value - log_total) / math.log(VOCAB))
    centres = jnp.arange(BINS, dtype=jnp.float32) + 0.5
    exit_bins = jnp.maximum(0.0, 1.0 - jnp.abs(bin_place[:, None] - centres[None, :]))
    prompt_ids = jnp.arange(PROMPTS, dtype=jnp.int32)
    leaving = jnp.any(prompt_ids[:, None] == exit_ids[None, :], axis=1)
    sorting_key = jnp.where(leaving, PROMPTS * N_DP + prompt_ids, destination * PROMPTS + prompt_ids)
    sorted_order = jnp.argsort(sorting_key)[:SURVIVING_COUNT].astype(jnp.int32)
    moved_rows = jnp.take(hidden, sorted_order, axis=0)
    return (exit_nll, exit_bins, moved_rows)
```

```python
import functools
import math

import jax
import jax.numpy as jnp
from jax import lax
from jax.experimental import pallas as pl
from jax.experimental.pallas import tpu as pltpu
from jax.sharding import PartitionSpec as P

BINS = 15
EPSILON = 1e-06
PACK = 16
CHUNK = 16
MESH = pl.DeviceIdType.MESH


def partner_of(me, bit):
    return me + (1 - 2 * ((me // (1 << bit)) % 2)) * (1 << bit)


def block_of(me, mask, bits):
    for bit in range(bits):
        if mask >> bit & 1:
            me = partner_of(me, bit)
    return me


def kernel(
    n,
    per,
    hidden,
    weight,
    gain,
    label_row,
    exit_ids,
    destination,
    moved,
    result,
    held,
    weights,
    raw,
    rows,
    outgoing,
    incoming,
    staged,
    stats,
    arrived,
    load_sem,
    weight_sem,
    row_send,
    row_recv,
    big_send,
    big_recv,
    stat_send,
    stat_recv,
    out_sem,
):
    me = lax.axis_index("dp")
    bits = n.bit_length() - 1
    parts = PACK // per
    width = hidden.shape[2] // parts
    pieces = len(held)
    vocab = weight.shape[1]
    vocab_total = vocab * n

    barrier = pltpu.get_barrier_semaphore()

    def greet(k, carry):
        pl.semaphore_signal(
            barrier, inc=1, device_id={"dp": (me + k) % n}, device_id_type=MESH
        )
        return carry

    loads = {}
    order = [pieces - 1] + list(range(pieces - 1))
    for c in order:
        loads[c] = pltpu.make_async_copy(
            hidden.at[:, pl.ds(c * CHUNK, CHUNK), :], held[c], load_sem.at[c]
        )
        loads[c].start()
    lax.fori_loop(1, n, greet, 0)
    weight_copy = pltpu.make_async_copy(weight, weights, weight_sem)
    weight_copy.start()

    loads[pieces - 1].wait()
    for p in range(per):
        row = held[pieces - 1][p, CHUNK - 8 : CHUNK, :].astype(jnp.float32)[7:8, :]
        for q in range(parts):
            raw[q * per + p : q * per + p + 1, :] = row[:, q * width : (q + 1) * width]
    values = raw[...]
    squares = jnp.sum(values * values, axis=1, keepdims=True)
    squares = jnp.broadcast_to(squares, (PACK, 128))
    shift = per
    while shift < PACK:
        squares = squares + pltpu.roll(squares, shift, 0)
        shift *= 2
    scale = lax.rsqrt(squares[:, :1] / hidden.shape[2] + EPSILON)
    part_of = lax.broadcasted_iota(jnp.int32, (PACK, width), 0) // per
    gains = jnp.zeros((PACK, width), jnp.float32)
    for q in range(parts):
        gains = jnp.where(part_of == q, gain[:, q * width : (q + 1) * width], gains)
    rows[me] = (values * scale * gains).astype(jnp.bfloat16)

    pl.semaphore_wait(barrier, n - 1)

    bit_order = list(range(1, bits)) + [0]
    sent = []

    def send_stage(stage, have):
        bit = bit_order[stage]
        new = []
        for mask in have:
            j = block_of(me, mask, bits)
            to = mask ^ (1 << bit)
            if mask:
                got(mask)
            copy = pltpu.make_async_remote_copy(
                src_ref=rows.at[j],
                dst_ref=rows.at[j],
                send_sem=row_send.at[to],
                recv_sem=row_recv.at[to],
                device_id={"dp": partner_of(me, bit)},
                device_id_type=MESH,
            )
            copy.start()
            sent.append(copy)
            new.append(to)
        return have + new

    seen = set()

    def got(mask):
        if mask in seen:
            return
        seen.add(mask)
        j = block_of(me, mask, bits)
        pltpu.make_async_remote_copy(
            src_ref=rows.at[j],
            dst_ref=rows.at[j],
            send_sem=row_send.at[mask],
            recv_sem=row_recv.at[mask],
            device_id={"dp": partner_of(me, 0)},
            device_id_type=MESH,
        ).wait_recv()

    have = send_stage(0, [0])

    target = [destination[me * per + i] for i in range(per)]
    to_right = jnp.int32(0)
    to_left = jnp.int32(0)
    for i in range(1, per):
        to_right = jnp.where(target[i] == me + 1, i, to_right)
        to_left = jnp.where(target[i] == me - 1, i, to_left)
    chosen = (to_right, to_left)
    can_send = (me < n - 1, me > 0)
    can_receive = (me > 0, me < n - 1)

    def big_copy(side, c):
        other = jnp.clip(me + 1 - 2 * side, 0, n - 1)
        return pltpu.make_async_remote_copy(
            src_ref=outgoing.at[side, c],
            dst_ref=incoming.at[side, c],
            send_sem=big_send.at[side, c],
            recv_sem=big_recv.at[side, c],
            device_id={"dp": other},
            device_id_type=MESH,
        )

    for c in order:
        if c != pieces - 1:
            loads[c].wait()
        for side in range(2):
            outgoing[side, c] = held[c][chosen[side]]

            @pl.when(can_send[side])
            def _():
                big_copy(side, c).start()

    for stage in range(1, bits):
        have = send_stage(stage, have)

    count = exit_ids.shape[0]

    def lookup(k, leaving):
        e = exit_ids[k] - me * per
        return tuple(jnp.where(e == i, 1, leaving[i]) for i in range(per))

    leaving = lax.fori_loop(0, count, lookup, (jnp.int32(0),) * per)
    first = jnp.int32(0)
    last = jnp.int32(0)
    for i in range(per):
        last = jnp.where((target[i] == me) & (leaving[i] == 0), i, last)
        k = per - 1 - i
        first = jnp.where((target[k] == me) & (leaving[k] == 0), k, first)
    before = jnp.maximum(me - 1, 0) * per
    after = jnp.minimum(me + 1, n - 1) * per
    from_left = jnp.int32(0)
    from_right = jnp.int32(0)
    for i in range(per):
        from_left = jnp.where(destination[before + i] == me, 1, from_left)
        from_right = jnp.where(destination[after + i] == me, 1, from_right)
    from_left = jnp.where(me > 0, from_left, 0)
    from_right = jnp.where(me < n - 1, from_right, 0)

    weight_copy.wait()
    for mask in range(1, n):
        got(mask)
    group = min(n, 16)
    high = group * PACK
    every = label_row.shape[1]

    def block(b, carry):
        held_rows = rows[pl.ds(b * group, group)].reshape(high, width)
        row_id = lax.broadcasted_iota(jnp.int32, (high, vocab), 0)
        row_part = (row_id // per) % parts
        logits = jnp.zeros((high, vocab), jnp.float32)
        for q in range(parts):
            product = jnp.dot(
                held_rows,
                weights[q * width : (q + 1) * width, :],
                preferred_element_type=jnp.float32,
            )
            logits = jnp.where(row_part == q, product, logits)
        shift = per
        while shift < PACK:
            logits = logits + pltpu.roll(logits, shift, 0)
            shift *= 2
        peak = jnp.max(logits, axis=1, keepdims=True)
        total = jnp.sum(jnp.exp(logits - peak), axis=1, keepdims=True)
        r = lax.broadcasted_iota(jnp.int32, (high, every), 0)
        prompt = (b * group + r // PACK) * per + r % per
        column = lax.broadcasted_iota(jnp.int32, (high, every), 1)
        label = jnp.sum(
            jnp.where(column == prompt, label_row[...].astype(jnp.float32), 0.0),
            axis=1,
            keepdims=True,
        )
        ids = lax.broadcasted_iota(jnp.int32, (high, vocab), 1) + me * vocab
        picked = jnp.sum(
            jnp.where(ids.astype(jnp.float32) == label, logits, 0.0), axis=1, keepdims=True
        )
        lane = lax.broadcasted_iota(jnp.int32, (high, 128), 1)
        packed = jnp.where(lane == 0, peak, jnp.where(lane == 1, total, picked))
        stats[pl.ds(b * group, group)] = packed.reshape(group, PACK, 128)[:, PACK - 8 :, :]
        return carry

    if n == group:
        block(0, 0)
    else:
        lax.fori_loop(0, n // group, block, 0)

    def stat_copy(k, source):
        other = (me + k) % n
        return pltpu.make_async_remote_copy(
            src_ref=stats.at[other],
            dst_ref=arrived.at[source],
            send_sem=stat_send.at[k],
            recv_sem=stat_recv.at[k],
            device_id={"dp": other},
            device_id_type=MESH,
        )

    def stat_start(k, carry):
        stat_copy(k, me).start()
        return carry

    lax.fori_loop(1, n, stat_start, 0)
    arrived[me] = stats[me]

    gets = (from_left, from_right)
    keeps = (first, last)
    for c in order:
        for side in range(2):

            @pl.when(can_receive[side])
            def _():
                big_copy(side, c).wait_recv()

            own = held[c][keeps[side]]
            staged[side, c] = jnp.where(gets[side] > 0, incoming[side, c], own)
            pltpu.make_async_copy(
                staged.at[side, c],
                moved.at[side, pl.ds(c * CHUNK, CHUNK), :],
                out_sem.at[side, c],
            ).start()

    def stat_wait(k, carry):
        stat_copy(k, (me + n - k) % n).wait_recv()
        return carry

    lax.fori_loop(1, n, stat_wait, 0)
    everything = arrived[...]
    peaks = everything[:, :, 0:1]
    peak = jnp.max(peaks, axis=0)
    total = jnp.sum(everything[:, :, 1:2] * jnp.exp(peaks - peak[None]), axis=0)
    picked = jnp.sum(everything[:, :, 2:3], axis=0)
    log_total = peak + jnp.log(total)
    nll = log_total - picked
    place = BINS * (1.0 + (peak - log_total) / math.log(vocab_total))
    lane = lax.broadcasted_iota(jnp.int32, (8, 128), 1)
    centre = lane.astype(jnp.float32) + 0.5
    bins = jnp.maximum(0.0, 1.0 - jnp.abs(place - centre))
    result[...] = jnp.where(lane < BINS, bins, nll)

    for c in order:
        for side in range(2):
            pltpu.make_async_copy(
                staged.at[side, c],
                moved.at[side, pl.ds(c * CHUNK, CHUNK), :],
                out_sem.at[side, c],
            ).wait()

            @pl.when(can_send[side])
            def _():
                big_copy(side, c).wait_send()

    for copy in sent:
        copy.wait_send()

    def stat_done(k, carry):
        stat_copy(k, me).wait_send()
        return carry

    lax.fori_loop(1, n, stat_done, 0)


def shards(hidden, exit_gain, exit_weight, labels, exit_ids, destination):
    n = lax.axis_size("dp")
    per, length, depth = hidden.shape
    vocab = exit_weight.shape[1]
    pieces = length // CHUNK
    slots = per // 2
    width = depth // (PACK // per)
    hbm = pl.BlockSpec(memory_space=pl.ANY)
    vmem = pl.BlockSpec(memory_space=pltpu.VMEM)
    smem = pl.BlockSpec(memory_space=pltpu.SMEM)
    bf16 = jnp.bfloat16
    moved, result = pl.pallas_call(
        lambda *refs: kernel(n, per, *refs),
        out_shape=(
            jax.ShapeDtypeStruct((slots, length, depth), bf16),
            jax.ShapeDtypeStruct((8, 128), jnp.float32),
        ),
        in_specs=[hbm, hbm, vmem, vmem, smem, smem],
        out_specs=(hbm, vmem),
        scratch_shapes=[
            [pltpu.VMEM((per, CHUNK, depth), bf16) for _ in range(pieces)],
            pltpu.VMEM((depth, vocab), bf16),
            pltpu.VMEM((PACK, width), jnp.float32),
            pltpu.VMEM((n, PACK, width), bf16),
            pltpu.VMEM((2, pieces, CHUNK, depth), bf16),
            pltpu.VMEM((2, pieces, CHUNK, depth), bf16),
            pltpu.VMEM((2, pieces, CHUNK, depth), bf16),
            pltpu.VMEM((n, 8, 128), jnp.float32),
            pltpu.VMEM((n, 8, 128), jnp.float32),
            pltpu.SemaphoreType.DMA((pieces,)),
            pltpu.SemaphoreType.DMA,
            pltpu.SemaphoreType.DMA((n,)),
            pltpu.SemaphoreType.DMA((n,)),
            pltpu.SemaphoreType.DMA((2, pieces)),
            pltpu.SemaphoreType.DMA((2, pieces)),
            pltpu.SemaphoreType.DMA((n,)),
            pltpu.SemaphoreType.DMA((n,)),
            pltpu.SemaphoreType.DMA((2, pieces)),
        ],
        compiler_params=pltpu.CompilerParams(
            collective_id=0, has_side_effects=True, vmem_limit_bytes=56 * 1024 * 1024
        ),
    )(
        hidden,
        exit_weight,
        exit_gain.reshape(1, depth),
        labels.reshape(1, -1),
        exit_ids,
        destination,
    )
    valid = result[8 - per :]
    return valid[:, 127], valid[:, :BINS], moved


def solution(mesh):
    in_specs = (
        P(("groups", "dp"), None, None),
        P(),
        P(None, "dp"),
        P("groups"),
        P("groups"),
        P("groups"),
    )
    out_specs = (P(("groups", "dp")), P(("groups", "dp"), None), P(("groups", "dp"), None, None))
    return jax.shard_map(shards, mesh=mesh, in_specs=in_specs, out_specs=out_specs, check_vma=False)
```

```python
import functools
import math

import jax
import jax.numpy as jnp
from jax import lax
from jax.experimental import pallas as pl
from jax.experimental.pallas import tpu as pltpu
from jax.sharding import PartitionSpec as P

BINS = 15
EPSILON = 1e-06
PACK = 16
CHUNK = 16
LATER = 1
MESH = pl.DeviceIdType.MESH


def partner_of(me, bit):
    return me + (1 - 2 * ((me // (1 << bit)) % 2)) * (1 << bit)


def kernel(
    n,
    per,
    hidden,
    weight,
    gain,
    label_row,
    exit_ids,
    destination,
    moved,
    result,
    held,
    weights,
    raw,
    rows,
    outgoing,
    incoming,
    stats,
    arrived,
    load_sem,
    weight_sem,
    row_send,
    row_recv,
    big_send,
    big_recv,
    stat_send,
    stat_recv,
):
    me = lax.axis_index("dp")
    parts = PACK // per
    width = hidden.shape[2] // parts
    pieces = len(held)
    vocab = weight.shape[1]
    vocab_total = vocab * n

    barrier = pltpu.get_barrier_semaphore()

    def greet(k, carry):
        pl.semaphore_signal(
            barrier, inc=1, device_id={"dp": (me + k) % n}, device_id_type=MESH
        )
        return carry

    loads = {}
    order = [pieces - 1] + list(range(pieces - 1))
    for c in order:
        loads[c] = pltpu.make_async_copy(
            hidden.at[:, pl.ds(c * CHUNK, CHUNK), :], held[c], load_sem.at[c]
        )
        loads[c].start()
    lax.fori_loop(1, n, greet, 0)
    weight_copy = pltpu.make_async_copy(weight, weights, weight_sem)
    weight_copy.start()

    loads[pieces - 1].wait()
    for p in range(per):
        row = held[pieces - 1][p, CHUNK - 8 : CHUNK, :].astype(jnp.float32)[7:8, :]
        for q in range(parts):
            raw[q * per + p : q * per + p + 1, :] = row[:, q * width : (q + 1) * width]
    values = raw[...]
    squares = jnp.sum(values * values, axis=1, keepdims=True)
    squares = jnp.broadcast_to(squares, (PACK, 128))
    shift = per
    while shift < PACK:
        squares = squares + pltpu.roll(squares, shift, 0)
        shift *= 2
    scale = lax.rsqrt(squares[:, :1] / hidden.shape[2] + EPSILON)
    part_of = lax.broadcasted_iota(jnp.int32, (PACK, width), 0) // per
    gains = jnp.zeros((PACK, width), jnp.float32)
    for q in range(parts):
        gains = jnp.where(part_of == q, gain[:, q * width : (q + 1) * width], gains)
    rows[me // 4, (me // 2) % 2, me % 2] = (values * scale * gains).astype(jnp.bfloat16)

    pl.semaphore_wait(barrier, n - 1)

    layers = n // 4
    layer, core = me // 4, me % 2
    top = layers - 1

    def row_copy(ref, sem, other):
        return pltpu.make_async_remote_copy(
            src_ref=ref,
            dst_ref=ref,
            send_sem=row_send.at[sem],
            recv_sem=row_recv.at[sem],
            device_id={"dp": other},
            device_id_type=MESH,
        )

    my_y = (me // 2) % 2
    ys = (my_y, 1 - my_y)
    both = range(2)

    def along_y(b):
        return row_copy(rows.at[layer, ys[b], core], 0, partner_of(me, 1))

    def upward(unit, step, b):
        other = jnp.minimum(me + 4, n - 4 + me % 4)
        return row_copy(rows.at[unit, ys[b], core], 1 + 2 * step + b, other)

    def downward(unit, step, b):
        other = jnp.maximum(me - 4, me % 4)
        return row_copy(rows.at[unit, ys[b], core], 1 + 2 * top + 2 * step + b, other)

    def across(unit, side, slot, b):
        sem = 1 + 4 * top + 2 * slot + b
        return row_copy(rows.at[unit, ys[b], side], sem, partner_of(me, 0))

    def launch(step, b):
        @pl.when((layer >= step) & (layer < top))
        def _():
            upward(layer - step, step, b).start()

        @pl.when((layer + step <= top) & (layer > 0))
        def _():
            downward(layer + step, step, b).start()

    def take(step, b):
        @pl.when(layer - 1 - step >= 0)
        def _():
            upward(layer - 1 - step, step, b).wait_recv()
            across(layer - 1 - step, core, 1 + step, b).start()

        @pl.when(layer + 1 + step <= top)
        def _():
            downward(layer + 1 + step, step, b).wait_recv()
            across(layer + 1 + step, core, top + 1 + step, b).start()

    along_y(0).start()
    launch(0, 0)
    across(layer, core, 0, 0).start()

    target = [destination[me * per + i] for i in range(per)]
    to_right = jnp.int32(0)
    to_left = jnp.int32(0)
    for i in range(1, per):
        to_right = jnp.where(target[i] == me + 1, i, to_right)
        to_left = jnp.where(target[i] == me - 1, i, to_left)
    chosen = (to_right, to_left)
    can_send = (me < n - 1, me > 0)
    far = (me % 4 == 3, me % 4 == 0)
    near = (me % 4 != 3, me % 4 != 0)
    can_receive = (me > 0, me < n - 1)

    def big_copy(side, c):
        other = jnp.clip(me + 1 - 2 * side, 0, n - 1)
        return pltpu.make_async_remote_copy(
            src_ref=outgoing.at[side, c],
            dst_ref=incoming.at[side, c],
            send_sem=big_send.at[side, c],
            recv_sem=big_recv.at[side, c],
            device_id={"dp": other},
            device_id_type=MESH,
        )

    for c in order:
        if c != pieces - 1:
            loads[c].wait()
        for side in range(2):
            outgoing[side, c] = held[c][chosen[side]]

            @pl.when(can_send[side] & near[side])
            def _():
                big_copy(side, c).start()

    along_y(1).wait_recv()
    launch(0, 1)
    across(layer, core, 0, 1).start()
    for step in range(top):
        for b in both:
            take(step, b)
            if step + 1 < top:
                launch(step + 1, b)
        if step == min(LATER, top - 1):
            for c in order:
                for side in range(2):

                    @pl.when(can_send[side] & far[side])
                    def _():
                        big_copy(side, c).start()

    count = exit_ids.shape[0]

    def lookup(k, leaving):
        e = exit_ids[k] - me * per
        return tuple(jnp.where(e == i, 1, leaving[i]) for i in range(per))

    leaving = lax.fori_loop(0, count, lookup, (jnp.int32(0),) * per)
    first = jnp.int32(0)
    last = jnp.int32(0)
    for i in range(per):
        last = jnp.where((target[i] == me) & (leaving[i] == 0), i, last)
        k = per - 1 - i
        first = jnp.where((target[k] == me) & (leaving[k] == 0), k, first)
    before = jnp.maximum(me - 1, 0) * per
    after = jnp.minimum(me + 1, n - 1) * per
    from_left = jnp.int32(0)
    from_right = jnp.int32(0)
    for i in range(per):
        from_left = jnp.where(destination[before + i] == me, 1, from_left)
        from_right = jnp.where(destination[after + i] == me, 1, from_right)
    from_left = jnp.where(me > 0, from_left, 0)
    from_right = jnp.where(me < n - 1, from_right, 0)

    weight_copy.wait()
    for b in both:
        across(layer, 1 - core, 0, b).wait_recv()
        for step in range(top):

            @pl.when(layer - 1 - step >= 0)
            def _():
                across(layer - 1 - step, 1 - core, 1 + step, b).wait_recv()

            @pl.when(layer + 1 + step <= top)
            def _():
                across(layer + 1 + step, 1 - core, top + 1 + step, b).wait_recv()

    group = min(n, 16)
    high = group * PACK
    every = label_row.shape[1]

    def block(b, carry):
        held_rows = rows[pl.ds(b * (group // 4), group // 4)].reshape(high, width)
        row_id = lax.broadcasted_iota(jnp.int32, (high, vocab), 0)
        row_part = (row_id // per) % parts
        logits = jnp.zeros((high, vocab), jnp.float32)
        for q in range(parts):
            product = jnp.dot(
                held_rows,
                weights[q * width : (q + 1) * width, :],
                preferred_element_type=jnp.float32,
            )
            logits = jnp.where(row_part == q, product, logits)
        shift = per
        while shift < PACK:
            logits = logits + pltpu.roll(logits, shift, 0)
            shift *= 2
        peak = jnp.max(logits, axis=1, keepdims=True)
        total = jnp.sum(jnp.exp(logits - peak), axis=1, keepdims=True)
        r = lax.broadcasted_iota(jnp.int32, (high, every), 0)
        prompt = (b * group + r // PACK) * per + r % per
        column = lax.broadcasted_iota(jnp.int32, (high, every), 1)
        label = jnp.sum(
            jnp.where(column == prompt, label_row[...].astype(jnp.float32), 0.0),
            axis=1,
            keepdims=True,
        )
        ids = lax.broadcasted_iota(jnp.int32, (high, vocab), 1) + me * vocab
        picked = jnp.sum(
            jnp.where(ids.astype(jnp.float32) == label, logits, 0.0), axis=1, keepdims=True
        )
        lane = lax.broadcasted_iota(jnp.int32, (high, 128), 1)
        packed = jnp.where(lane == 0, peak, jnp.where(lane == 1, total, picked))
        stats[pl.ds(b * group, group)] = packed.reshape(group, PACK, 128)[:, PACK - 8 :, :]
        return carry

    if n == group:
        block(0, 0)
    else:
        lax.fori_loop(0, n // group, block, 0)

    def stat_copy(k, source):
        other = (me + k) % n
        return pltpu.make_async_remote_copy(
            src_ref=stats.at[other],
            dst_ref=arrived.at[source],
            send_sem=stat_send.at[k],
            recv_sem=stat_recv.at[k],
            device_id={"dp": other},
            device_id_type=MESH,
        )

    def stat_start(k, carry):
        stat_copy(k, me).start()
        return carry

    lax.fori_loop(1, n, stat_start, 0)
    arrived[me] = stats[me]

    gets = (from_left, from_right)
    keeps = (first, last)
    for c in order:
        for side in range(2):

            @pl.when(can_receive[side])
            def _():
                big_copy(side, c).wait_recv()

            own = held[c][keeps[side]]
            moved[side, c * CHUNK : (c + 1) * CHUNK, :] = jnp.where(
                gets[side] > 0, incoming[side, c], own
            )

    def stat_wait(k, carry):
        stat_copy(k, (me + n - k) % n).wait_recv()
        return carry

    lax.fori_loop(1, n, stat_wait, 0)
    everything = arrived[...]
    peaks = everything[:, :, 0:1]
    peak = jnp.max(peaks, axis=0)
    total = jnp.sum(everything[:, :, 1:2] * jnp.exp(peaks - peak[None]), axis=0)
    picked = jnp.sum(everything[:, :, 2:3], axis=0)
    log_total = peak + jnp.log(total)
    nll = log_total - picked
    place = BINS * (1.0 + (peak - log_total) / math.log(vocab_total))
    lane = lax.broadcasted_iota(jnp.int32, (8, 128), 1)
    centre = lane.astype(jnp.float32) + 0.5
    bins = jnp.maximum(0.0, 1.0 - jnp.abs(place - centre))
    result[0:8, :] = bins
    row = lax.broadcasted_iota(jnp.int32, (8, 128), 0)
    nll_row = jnp.sum(jnp.where(lane == row - (8 - per), nll, 0.0), axis=0, keepdims=True)
    result[8:16, :] = jnp.broadcast_to(nll_row, (8, 128))

    for c in order:
        for side in range(2):

            @pl.when(can_send[side])
            def _():
                big_copy(side, c).wait_send()

    along_y(0).wait_send()
    for b in both:
        across(layer, core, 0, b).wait_send()
        for step in range(top):

            @pl.when((layer >= step) & (layer < top))
            def _():
                upward(layer - step, step, b).wait_send()

            @pl.when((layer + step <= top) & (layer > 0))
            def _():
                downward(layer + step, step, b).wait_send()

            @pl.when(layer - 1 - step >= 0)
            def _():
                across(layer - 1 - step, core, 1 + step, b).wait_send()

            @pl.when(layer + 1 + step <= top)
            def _():
                across(layer + 1 + step, core, top + 1 + step, b).wait_send()

    def stat_done(k, carry):
        stat_copy(k, me).wait_send()
        return carry

    lax.fori_loop(1, n, stat_done, 0)


def finish(moved, result, nll, bins, out, sems):
    copies = []
    for k in range(sems.shape[0]):
        copies.append(pltpu.make_async_copy(moved.at[k], out.at[k], sems.at[k]))
        copies[-1].start()
    per = bins.shape[0]
    nll[...] = result[8:9, 0:per]
    bins[...] = result[8 - per : 8, 0:BINS]
    for copy in copies:
        copy.wait()


def shards(hidden, exit_gain, exit_weight, labels, exit_ids, destination):
    n = lax.axis_size("dp")
    per, length, depth = hidden.shape
    vocab = exit_weight.shape[1]
    pieces = length // CHUNK
    slots = per // 2
    width = depth // (PACK // per)
    hbm = pl.BlockSpec(memory_space=pl.ANY)
    pinned = pl.BlockSpec(memory_space=pltpu.HBM)
    vmem = pl.BlockSpec(memory_space=pltpu.VMEM)
    smem = pl.BlockSpec(memory_space=pltpu.SMEM)
    bf16 = jnp.bfloat16
    moved, result = pl.pallas_call(
        lambda *refs: kernel(n, per, *refs),
        out_shape=(
            pltpu.VMEM((slots, length, depth), bf16),
            pltpu.VMEM((16, 128), jnp.float32),
        ),
        in_specs=[pinned, pinned, vmem, vmem, smem, smem],
        out_specs=(vmem, vmem),
        scratch_shapes=[
            [pltpu.VMEM((per, CHUNK, depth), bf16) for _ in range(pieces)],
            pltpu.VMEM((depth, vocab), bf16),
            pltpu.VMEM((PACK, width), jnp.float32),
            pltpu.VMEM((n // 4, 2, 2, PACK, width), bf16),
            pltpu.VMEM((2, pieces, CHUNK, depth), bf16),
            pltpu.VMEM((2, pieces, CHUNK, depth), bf16),
            pltpu.VMEM((n, 8, 128), jnp.float32),
            pltpu.VMEM((n, 8, 128), jnp.float32),
            pltpu.SemaphoreType.DMA((pieces,)),
            pltpu.SemaphoreType.DMA,
            pltpu.SemaphoreType.DMA((2 * n,)),
            pltpu.SemaphoreType.DMA((2 * n,)),
            pltpu.SemaphoreType.DMA((2, pieces)),
            pltpu.SemaphoreType.DMA((2, pieces)),
            pltpu.SemaphoreType.DMA((n,)),
            pltpu.SemaphoreType.DMA((n,)),
        ],
        compiler_params=pltpu.CompilerParams(
            collective_id=0, has_side_effects=True, vmem_limit_bytes=56 * 1024 * 1024
        ),
    )(
        hidden,
        exit_weight,
        exit_gain.reshape(1, depth),
        labels.reshape(1, -1),
        exit_ids,
        destination,
    )
    nll, bins, placed = pl.pallas_call(
        finish,
        out_shape=(
            jax.ShapeDtypeStruct((1, per), jnp.float32),
            jax.ShapeDtypeStruct((per, BINS), jnp.float32),
            jax.ShapeDtypeStruct((slots, length, depth), bf16),
        ),
        in_specs=[hbm, vmem],
        out_specs=(vmem, vmem, hbm),
        scratch_shapes=[pltpu.SemaphoreType.DMA((slots,))],
        compiler_params=pltpu.CompilerParams(vmem_limit_bytes=2 * 1024 * 1024),
    )(moved, result)
    return nll.reshape(per), bins, placed


def solution(mesh):
    in_specs = (
        P(("groups", "dp"), None, None),
        P(),
        P(None, "dp"),
        P("groups"),
        P("groups"),
        P("groups"),
    )
    out_specs = (P(("groups", "dp")), P(("groups", "dp"), None), P(("groups", "dp"), None, None))
    return jax.shard_map(shards, mesh=mesh, in_specs=in_specs, out_specs=out_specs, check_vma=False)
```

```python
import functools
import math

import jax
import jax.numpy as jnp
from jax import lax
from jax.experimental import pallas as pl
from jax.experimental.pallas import tpu as pltpu
from jax.sharding import PartitionSpec as P

BINS = 15
EPSILON = 1e-06
PACK = 16
CHUNK = 32
LATER = 1
MESH = pl.DeviceIdType.MESH


def partner_of(me, bit):
    return me + (1 - 2 * ((me // (1 << bit)) % 2)) * (1 << bit)


def kernel(
    n,
    per,
    hidden,
    weight,
    gain,
    label_row,
    exit_ids,
    destination,
    moved,
    result,
    held,
    weights,
    raw,
    rows,
    outgoing,
    incoming,
    stats,
    arrived,
    load_sem,
    weight_sem,
    row_send,
    row_recv,
    big_send,
    big_recv,
    stat_send,
    stat_recv,
):
    me = lax.axis_index("dp")
    parts = PACK // per
    width = hidden.shape[2] // parts
    pieces = len(held)
    vocab = weight.shape[1]
    vocab_total = vocab * n

    barrier = pltpu.get_barrier_semaphore()

    def greet(k, carry):
        pl.semaphore_signal(
            barrier, inc=1, device_id={"dp": (me + k) % n}, device_id_type=MESH
        )
        return carry

    loads = {}
    order = [pieces - 1] + list(range(pieces - 1))
    for c in order:
        loads[c] = pltpu.make_async_copy(
            hidden.at[:, pl.ds(c * CHUNK, CHUNK), :], held[c], load_sem.at[c]
        )
        loads[c].start()
    lax.fori_loop(1, n, greet, 0)
    weight_copy = pltpu.make_async_copy(weight, weights, weight_sem)
    weight_copy.start()

    loads[pieces - 1].wait()
    for p in range(per):
        row = held[pieces - 1][p, CHUNK - 8 : CHUNK, :].astype(jnp.float32)[7:8, :]
        for q in range(parts):
            raw[q * per + p : q * per + p + 1, :] = row[:, q * width : (q + 1) * width]
    values = raw[...]
    squares = jnp.sum(values * values, axis=1, keepdims=True)
    squares = jnp.broadcast_to(squares, (PACK, 128))
    shift = per
    while shift < PACK:
        squares = squares + pltpu.roll(squares, shift, 0)
        shift *= 2
    scale = lax.rsqrt(squares[:, :1] / hidden.shape[2] + EPSILON)
    part_of = lax.broadcasted_iota(jnp.int32, (PACK, width), 0) // per
    gains = jnp.zeros((PACK, width), jnp.float32)
    for q in range(parts):
        gains = jnp.where(part_of == q, gain[:, q * width : (q + 1) * width], gains)
    rows[me // 4, (me // 2) % 2, me % 2] = (values * scale * gains).astype(jnp.bfloat16)

    pl.semaphore_wait(barrier, n - 1)

    layers = n // 4
    layer, core = me // 4, me % 2
    top = layers - 1

    def row_copy(ref, sem, other):
        return pltpu.make_async_remote_copy(
            src_ref=ref,
            dst_ref=ref,
            send_sem=row_send.at[sem],
            recv_sem=row_recv.at[sem],
            device_id={"dp": other},
            device_id_type=MESH,
        )

    my_y = (me // 2) % 2
    ys = (my_y, 1 - my_y)
    both = range(2)

    def along_y(b):
        return row_copy(rows.at[layer, ys[b], core], 0, partner_of(me, 1))

    def upward(unit, step, b):
        other = jnp.minimum(me + 4, n - 4 + me % 4)
        return row_copy(rows.at[unit, ys[b], core], 1 + 2 * step + b, other)

    def downward(unit, step, b):
        other = jnp.maximum(me - 4, me % 4)
        return row_copy(rows.at[unit, ys[b], core], 1 + 2 * top + 2 * step + b, other)

    def across(unit, side, slot, b):
        sem = 1 + 4 * top + 2 * slot + b
        return row_copy(rows.at[unit, ys[b], side], sem, partner_of(me, 0))

    def launch(step, b):
        @pl.when((layer >= step) & (layer < top))
        def _():
            upward(layer - step, step, b).start()

        @pl.when((layer + step <= top) & (layer > 0))
        def _():
            downward(layer + step, step, b).start()

    def take(step, b):
        @pl.when(layer - 1 - step >= 0)
        def _():
            upward(layer - 1 - step, step, b).wait_recv()
            across(layer - 1 - step, core, 1 + step, b).start()

        @pl.when(layer + 1 + step <= top)
        def _():
            downward(layer + 1 + step, step, b).wait_recv()
            across(layer + 1 + step, core, top + 1 + step, b).start()

    along_y(0).start()
    launch(0, 0)
    across(layer, core, 0, 0).start()

    target = [destination[me * per + i] for i in range(per)]
    to_right = jnp.int32(0)
    to_left = jnp.int32(0)
    for i in range(1, per):
        to_right = jnp.where(target[i] == me + 1, i, to_right)
        to_left = jnp.where(target[i] == me - 1, i, to_left)
    chosen = (to_right, to_left)
    can_send = (me < n - 1, me > 0)
    far = (me % 4 == 3, me % 4 == 0)
    near = (me % 4 != 3, me % 4 != 0)
    can_receive = (me > 0, me < n - 1)

    def big_copy(side, c):
        other = jnp.clip(me + 1 - 2 * side, 0, n - 1)
        return pltpu.make_async_remote_copy(
            src_ref=outgoing.at[side, c],
            dst_ref=incoming.at[side, c],
            send_sem=big_send.at[side, c],
            recv_sem=big_recv.at[side, c],
            device_id={"dp": other},
            device_id_type=MESH,
        )

    for c in order:
        if c != pieces - 1:
            loads[c].wait()
        for side in range(2):
            outgoing[side, c] = held[c][chosen[side]]

            @pl.when(can_send[side] & near[side])
            def _():
                big_copy(side, c).start()

    along_y(1).wait_recv()
    launch(0, 1)
    across(layer, core, 0, 1).start()
    for step in range(top):
        for b in both:
            take(step, b)
            if step + 1 < top:
                launch(step + 1, b)
        if step == min(LATER, top - 1):
            for c in order:
                for side in range(2):

                    @pl.when(can_send[side] & far[side])
                    def _():
                        big_copy(side, c).start()

    count = exit_ids.shape[0]

    def lookup(k, leaving):
        e = exit_ids[k] - me * per
        return tuple(jnp.where(e == i, 1, leaving[i]) for i in range(per))

    leaving = lax.fori_loop(0, count, lookup, (jnp.int32(0),) * per)
    first = jnp.int32(0)
    last = jnp.int32(0)
    for i in range(per):
        last = jnp.where((target[i] == me) & (leaving[i] == 0), i, last)
        k = per - 1 - i
        first = jnp.where((target[k] == me) & (leaving[k] == 0), k, first)
    before = jnp.maximum(me - 1, 0) * per
    after = jnp.minimum(me + 1, n - 1) * per
    from_left = jnp.int32(0)
    from_right = jnp.int32(0)
    for i in range(per):
        from_left = jnp.where(destination[before + i] == me, 1, from_left)
        from_right = jnp.where(destination[after + i] == me, 1, from_right)
    from_left = jnp.where(me > 0, from_left, 0)
    from_right = jnp.where(me < n - 1, from_right, 0)

    weight_copy.wait()
    for b in both:
        across(layer, 1 - core, 0, b).wait_recv()
        for step in range(top):

            @pl.when(layer - 1 - step >= 0)
            def _():
                across(layer - 1 - step, 1 - core, 1 + step, b).wait_recv()

            @pl.when(layer + 1 + step <= top)
            def _():
                across(layer + 1 + step, 1 - core, top + 1 + step, b).wait_recv()

    group = min(n, 16)
    high = group * PACK
    every = label_row.shape[1]

    def block(b, carry):
        held_rows = rows[pl.ds(b * (group // 4), group // 4)].reshape(high, width)
        row_id = lax.broadcasted_iota(jnp.int32, (high, vocab), 0)
        row_part = (row_id // per) % parts
        logits = jnp.zeros((high, vocab), jnp.float32)
        for q in range(parts):
            product = jnp.dot(
                held_rows,
                weights[q * width : (q + 1) * width, :],
                preferred_element_type=jnp.float32,
            )
            logits = jnp.where(row_part == q, product, logits)
        shift = per
        while shift < PACK:
            logits = logits + pltpu.roll(logits, shift, 0)
            shift *= 2
        peak = jnp.max(logits, axis=1, keepdims=True)
        total = jnp.sum(jnp.exp(logits - peak), axis=1, keepdims=True)
        r = lax.broadcasted_iota(jnp.int32, (high, every), 0)
        prompt = (b * group + r // PACK) * per + r % per
        column = lax.broadcasted_iota(jnp.int32, (high, every), 1)
        label = jnp.sum(
            jnp.where(column == prompt, label_row[...].astype(jnp.float32), 0.0),
            axis=1,
            keepdims=True,
        )
        ids = lax.broadcasted_iota(jnp.int32, (high, vocab), 1) + me * vocab
        picked = jnp.sum(
            jnp.where(ids.astype(jnp.float32) == label, logits, 0.0), axis=1, keepdims=True
        )
        lane = lax.broadcasted_iota(jnp.int32, (high, 128), 1)
        packed = jnp.where(lane == 0, peak, jnp.where(lane == 1, total, picked))
        stats[pl.ds(b * group, group)] = packed.reshape(group, PACK, 128)[:, PACK - 8 :, :]
        return carry

    if n == group:
        block(0, 0)
    else:
        lax.fori_loop(0, n // group, block, 0)

    def stat_copy(k, source):
        other = (me + k) % n
        return pltpu.make_async_remote_copy(
            src_ref=stats.at[other],
            dst_ref=arrived.at[source],
            send_sem=stat_send.at[k],
            recv_sem=stat_recv.at[k],
            device_id={"dp": other},
            device_id_type=MESH,
        )

    def stat_start(k, carry):
        stat_copy(k, me).start()
        return carry

    lax.fori_loop(1, n, stat_start, 0)
    arrived[me] = stats[me]

    gets = (from_left, from_right)
    keeps = (first, last)
    for c in order:
        for side in range(2):

            @pl.when(can_receive[side])
            def _():
                big_copy(side, c).wait_recv()

            own = held[c][keeps[side]]
            moved[side, c * CHUNK : (c + 1) * CHUNK, :] = jnp.where(
                gets[side] > 0, incoming[side, c], own
            )

    def stat_wait(k, carry):
        stat_copy(k, (me + n - k) % n).wait_recv()
        return carry

    lax.fori_loop(1, n, stat_wait, 0)
    everything = arrived[...]
    peaks = everything[:, :, 0:1]
    peak = jnp.max(peaks, axis=0)
    total = jnp.sum(everything[:, :, 1:2] * jnp.exp(peaks - peak[None]), axis=0)
    picked = jnp.sum(everything[:, :, 2:3], axis=0)
    log_total = peak + jnp.log(total)
    nll = log_total - picked
    place = BINS * (1.0 + (peak - log_total) / math.log(vocab_total))
    lane = lax.broadcasted_iota(jnp.int32, (8, 128), 1)
    centre = lane.astype(jnp.float32) + 0.5
    bins = jnp.maximum(0.0, 1.0 - jnp.abs(place - centre))
    result[0:8, :] = bins
    row = lax.broadcasted_iota(jnp.int32, (8, 128), 0)
    nll_row = jnp.sum(jnp.where(lane == row - (8 - per), nll, 0.0), axis=0, keepdims=True)
    result[8:16, :] = jnp.broadcast_to(nll_row, (8, 128))

    for c in order:
        for side in range(2):

            @pl.when(can_send[side])
            def _():
                big_copy(side, c).wait_send()

    along_y(0).wait_send()
    for b in both:
        across(layer, core, 0, b).wait_send()
        for step in range(top):

            @pl.when((layer >= step) & (layer < top))
            def _():
                upward(layer - step, step, b).wait_send()

            @pl.when((layer + step <= top) & (layer > 0))
            def _():
                downward(layer + step, step, b).wait_send()

            @pl.when(layer - 1 - step >= 0)
            def _():
                across(layer - 1 - step, core, 1 + step, b).wait_send()

            @pl.when(layer + 1 + step <= top)
            def _():
                across(layer + 1 + step, core, top + 1 + step, b).wait_send()

    def stat_done(k, carry):
        stat_copy(k, me).wait_send()
        return carry

    lax.fori_loop(1, n, stat_done, 0)


def finish(moved, result, nll, bins, out, sems):
    copies = []
    for k in range(sems.shape[0]):
        copies.append(pltpu.make_async_copy(moved.at[k], out.at[k], sems.at[k]))
        copies[-1].start()
    per = bins.shape[0]
    nll[...] = result[8:9, 0:per]
    bins[...] = result[8 - per : 8, 0:BINS]
    for copy in copies:
        copy.wait()


def shards(hidden, exit_gain, exit_weight, labels, exit_ids, destination):
    n = lax.axis_size("dp")
    per, length, depth = hidden.shape
    vocab = exit_weight.shape[1]
    pieces = length // CHUNK
    slots = per // 2
    width = depth // (PACK // per)
    hbm = pl.BlockSpec(memory_space=pl.ANY)
    pinned = pl.BlockSpec(memory_space=pltpu.HBM)
    vmem = pl.BlockSpec(memory_space=pltpu.VMEM)
    smem = pl.BlockSpec(memory_space=pltpu.SMEM)
    bf16 = jnp.bfloat16
    moved, result = pl.pallas_call(
        lambda *refs: kernel(n, per, *refs),
        out_shape=(
            pltpu.VMEM((slots, length, depth), bf16),
            pltpu.VMEM((16, 128), jnp.float32),
        ),
        in_specs=[pinned, pinned, vmem, vmem, smem, smem],
        out_specs=(vmem, vmem),
        scratch_shapes=[
            [pltpu.VMEM((per, CHUNK, depth), bf16) for _ in range(pieces)],
            pltpu.VMEM((depth, vocab), bf16),
            pltpu.VMEM((PACK, width), jnp.float32),
            pltpu.VMEM((n // 4, 2, 2, PACK, width), bf16),
            pltpu.VMEM((2, pieces, CHUNK, depth), bf16),
            pltpu.VMEM((2, pieces, CHUNK, depth), bf16),
            pltpu.VMEM((n, 8, 128), jnp.float32),
            pltpu.VMEM((n, 8, 128), jnp.float32),
            pltpu.SemaphoreType.DMA((pieces,)),
            pltpu.SemaphoreType.DMA,
            pltpu.SemaphoreType.DMA((2 * n,)),
            pltpu.SemaphoreType.DMA((2 * n,)),
            pltpu.SemaphoreType.DMA((2, pieces)),
            pltpu.SemaphoreType.DMA((2, pieces)),
            pltpu.SemaphoreType.DMA((n,)),
            pltpu.SemaphoreType.DMA((n,)),
        ],
        compiler_params=pltpu.CompilerParams(
            collective_id=0, has_side_effects=True, vmem_limit_bytes=56 * 1024 * 1024
        ),
    )(
        hidden,
        exit_weight,
        exit_gain.reshape(1, depth),
        labels.reshape(1, -1),
        exit_ids,
        destination,
    )
    nll, bins, placed = pl.pallas_call(
        finish,
        out_shape=(
            jax.ShapeDtypeStruct((1, per), jnp.float32),
            jax.ShapeDtypeStruct((per, BINS), jnp.float32),
            jax.ShapeDtypeStruct((slots, length, depth), bf16),
        ),
        in_specs=[hbm, vmem],
        out_specs=(vmem, vmem, hbm),
        scratch_shapes=[pltpu.SemaphoreType.DMA((slots,))],
        compiler_params=pltpu.CompilerParams(vmem_limit_bytes=2 * 1024 * 1024),
    )(moved, result)
    return nll.reshape(per), bins, placed


def solution(mesh):
    in_specs = (
        P(("groups", "dp"), None, None),
        P(),
        P(None, "dp"),
        P("groups"),
        P("groups"),
        P("groups"),
    )
    out_specs = (P(("groups", "dp")), P(("groups", "dp"), None), P(("groups", "dp"), None, None))
    return jax.shard_map(shards, mesh=mesh, in_specs=in_specs, out_specs=out_specs, check_vma=False)
```
